768 devices in a mesh: row: 192 (over z, y, core), col: 4 (over x).
Axes of the slice: x: 4, y: 8, z: 12, core: 2. Of those that a mesh axis runs over, the one named last changes fastest.
Arguments:
- features: bfloat16 [24576, 128], P(('row', 'col')), may hold values from -48 to 48
- tiles: bfloat16 [18432, 128, 128], P(('row', 'col')), may hold values from -0.0546875 to 0.0546875
- tile_rows: int32 [18432], P(('row', 'col')), may hold values from 0 to 47, as said below
- tile_count: int32 [768], P(('row', 'col')), may hold values from 1 to 24, as said below
- filters: bfloat16 [4, 128, 256], replicated, may hold values from -0.25 to 0.25
Outputs:
- normalized: bfloat16 [24576, 256], P(('row', 'col'))
The draws below stay inside these ranges and needn't reach their ends.
Inputs may be any that keep to these rules, and one draw needn't show every extreme that they name: `tile_rows`: slots at and beyond a device's count are padding. The row tiles named in one device's occupied slots are distinct. `tile_count`: some device has all 24 slots occupied.
All inputs are finite; a program needn't handle non-finite values.
Results may differ from the reference program's by a relative error of at most 0.009.
Values may be sent and summed in bfloat16 or wider, within the bound.
No kernel may reach another device: no remote copies, remote signals or barrier semaphores. Data moves between devices by JAX's collectives and lax.ppermute only.
A program may use at most 32 MiB of HBM per device.

```python
import math
import jax
import jax.numpy as jnp
from jax import lax

NODES_DEV = 32
TILE = 128
FIN = 128
HID = 256
CHEB = 4
NODES = 24576
BLOCK_COLS = 128
ROW_TILES = 48
SLOTS = 24
N_ROW = 192
N_COL = 4


def draw_features(key, part):
    key = jax.random.fold_in(key, 11)
    key_base, key_lift = jax.random.split(key, 2)
    position = jnp.arange(NODES, dtype=jnp.float32) / (NODES - 1)
    trend = 1.0 + 2.0 * position
    base = jax.random.normal(key_base, (NODES, FIN), jnp.float32)
    lift = jax.random.uniform(key_lift, (NODES, 1), jnp.float32, 0.0, math.log(10.0))
    return jnp.clip(0.3 * base * jnp.exp(lift) * trend[:, None], -48.0, 48.0).astype(jnp.bfloat16)


def draw_tile_rows(key, part):
    key = jax.random.fold_in(key, 23)
    device_keys = jax.random.split(key, N_ROW * N_COL)
    orders = jax.vmap(lambda single: jax.random.permutation(single, ROW_TILES))(device_keys)
    return orders[:, :SLOTS].reshape(-1).astype(jnp.int32)


def draw_tile_count(key, part):
    key = jax.random.fold_in(key, 37)
    key_first, key_second, key_top = jax.random.split(key, 3)
    devices = N_ROW * N_COL
    first = jax.random.randint(key_first, (devices,), 0, SLOTS + 1)
    second = jax.random.randint(key_second, (devices,), 0, SLOTS + 1)
    counts = jnp.maximum(SLOTS - first * second // SLOTS, 1)
    busiest = jax.random.randint(key_top, (), 0, devices)
    counts = jnp.where(jnp.arange(devices, dtype=jnp.int32) == busiest, SLOTS, counts)
    return counts.astype(jnp.int32)


def steps_of(rng, shape, cuts, low, high):
    loudness = 1.0
    for dim, parts in cuts:
        steps = jax.random.uniform(jax.random.fold_in(jax.random.fold_in(rng, 6), dim), (parts,), jnp.float32, low / len(cuts), high / len(cuts))
        loudness = loudness * jnp.repeat(jnp.exp(steps), shape[dim] // parts).reshape((-1,) + (1,) * (len(shape) - 1 - dim))
    return loudness


def centred(stream_key, dims, deviation, bound, pieces=(), held_as=jnp.bfloat16):
    factor_of = steps_of(stream_key, dims, pieces, -0.22, 0.18) if pieces else 1.0
    array = jax.random.normal(stream_key, dims, jnp.float32) * deviation * factor_of
    return jnp.minimum(jnp.maximum(array, -bound), bound).astype(held_as)


def setup_inputs(seed: int = 0) -> dict:
    key_of = jax.random.split(jax.random.key(seed), 6)
    return {
        "features": draw_features(jax.random.fold_in(key_of[5], 71), 0),
        "tiles": centred(key_of[1], (N_ROW * N_COL * SLOTS, TILE, BLOCK_COLS), (N_ROW * N_COL * NODES_DEV // 2) ** -0.5, 0.0546875, ((0, 768),)),
        "tile_rows": draw_tile_rows(jax.random.fold_in(key_of[5], 71), 0),
        "tile_count": draw_tile_count(jax.random.fold_in(key_of[5], 71), 0),
        "filters": centred(key_of[4], (CHEB, FIN, HID), (CHEB * FIN) ** -0.5, 0.25),
    }


epsilon = 1e-05

def propagate(vector, tiles, tile_rows, tile_count):
    width = vector.shape[1]
    devices = N_ROW * N_COL
    tile_sets = tiles.reshape(devices, SLOTS, TILE, BLOCK_COLS)
    slot_rows = tile_rows.reshape(devices, SLOTS)

    def add_device(running, item):
        tile_set, row_ids, occupied, device = item
        col_index = device % N_COL
        row_index = device // N_COL
        gathered = lax.dynamic_slice_in_dim(vector, (row_index * BLOCK_COLS).astype(jnp.int32), BLOCK_COLS, 0)
        products = jnp.einsum('sij,jf->sif', tile_set.astype(jnp.float32), gathered.astype(jnp.float32))
        in_use = jnp.arange(SLOTS, dtype=jnp.int32) < occupied
        select = ((row_ids[None, :] == jnp.arange(ROW_TILES, dtype=jnp.int32)[:, None]) & in_use[None, :]).astype(jnp.float32)
        block_sum = jnp.einsum('ts,sif->tif', select, products, precision=lax.Precision.HIGHEST)
        block_sum = block_sum.reshape(N_ROW, NODES_DEV, width)
        place = (jnp.arange(N_COL, dtype=jnp.int32) == col_index).astype(jnp.float32)
        running = running + block_sum[:, None] * place[None, :, None, None]
        return (running, None)
    start = jnp.zeros((N_ROW, N_COL, NODES_DEV, width), jnp.float32)
    running, unused = lax.scan(add_device, start, (tile_sets, slot_rows, tile_count, jnp.arange(devices, dtype=jnp.int32)))
    return running.reshape(NODES, width)

def reference(features, tiles, tile_rows, tile_count, filters):
    cheb_terms = [features]
    cheb_terms.append(propagate(features, tiles, tile_rows, tile_count).astype(jnp.bfloat16))
    for order in range(2, CHEB):
        image = propagate(cheb_terms[-1], tiles, tile_rows, tile_count)
        cheb_terms.append((2.0 * image - cheb_terms[-2].astype(jnp.float32)).astype(jnp.bfloat16))
    stacked = jnp.concatenate(cheb_terms, axis=1)
    hidden = jnp.dot(stacked, filters.reshape(CHEB * FIN, HID), preferred_element_type=jnp.float32)
    col_mean = lax.optimization_barrier(jnp.sum(hidden, axis=0)) / NODES
    centered = hidden - col_mean[None, :]
    spread = jnp.sum(centered * centered) / NODES
    return (centered * lax.rsqrt(spread + epsilon)).astype(jnp.bfloat16)
```

```python
import functools
import jax
import jax.numpy as jnp
from jax import lax
from jax.experimental import pallas as pl
from jax.experimental.pallas import tpu as pltpu
from jax.sharding import Mesh
from jax.sharding import PartitionSpec as P

VM = pl.BlockSpec(memory_space=pltpu.VMEM)
SM = pl.BlockSpec(memory_space=pltpu.SMEM)
epsilon = 1e-05
MODE = "yz"


def place_kernel(y_size, y_first, rows_ref, count_ref, tiles_ref, *out_refs):
    parts = len(out_refs)
    rows = out_refs[0].shape[3]
    pieces = tiles_ref.shape[1] // (rows * parts)
    for out_ref in out_refs:
        out_ref[...] = jnp.zeros_like(out_ref)

    def put(slot, carry):
        first = rows_ref[slot] * pieces
        for q in range(pieces):
            chip = (first + q) // 2
            y, z = chip % y_size, chip // y_size
            for part, out_ref in enumerate(out_refs):
                start = (q * parts + part) * rows
                place = (y, z) if y_first[part] else (z, y)
                out_ref[(first + q) % 2, place[0], place[1]] = tiles_ref[slot, start : start + rows, :]
        return carry

    lax.fori_loop(0, count_ref[0], put, 0)


def place(tiles, tile_rows, tile_count, z_size, y_size, piece, y_first):
    rows, cols = piece // len(y_first), tiles.shape[2]
    shapes = [(2, y_size, z_size, rows, cols) if y else (2, z_size, y_size, rows, cols) for y in y_first]
    return pl.pallas_call(
        functools.partial(place_kernel, y_size, y_first),
        out_shape=[jax.ShapeDtypeStruct(s, tiles.dtype) for s in shapes],
        in_specs=[SM, SM, VM],
        out_specs=[VM] * len(shapes),
        compiler_params=pltpu.CompilerParams(vmem_limit_bytes=16 * 1024 * 1024),
    )(tile_rows, tile_count, tiles)


def sum_kernel(in_ref, out_ref):
    for i in range(in_ref.shape[1]):
        total = in_ref[0, i].astype(jnp.float32)
        for source in range(1, in_ref.shape[0]):
            total = total + in_ref[source, i].astype(jnp.float32)
        total = total.astype(out_ref.dtype)
        for copy in range(out_ref.shape[1]):
            out_ref[i, copy] = total


def sum_sources(array, copies):
    return pl.pallas_call(
        sum_kernel,
        out_shape=jax.ShapeDtypeStruct((array.shape[1], copies) + array.shape[2:], array.dtype),
        in_specs=[VM],
        out_specs=VM,
    )(array)


def term_kernel(parts, scale, *refs):
    in_refs, prev_ref, out_ref = refs[:parts], (refs[parts] if scale != 1.0 else None), refs[-1]
    rows = in_refs[0].shape[2]
    for i in range(out_ref.shape[0]):
        for part, in_ref in enumerate(in_refs):
            total = in_ref[0, i].astype(jnp.float32)
            for source in range(1, in_ref.shape[0]):
                total = total + in_ref[source, i].astype(jnp.float32)
            at = slice(part * rows, (part + 1) * rows)
            if scale != 1.0:
                total = scale * total - prev_ref[i, at].astype(jnp.float32)
            out_ref[i, at] = total.astype(out_ref.dtype)


def next_term(parts, prev):
    operands = list(parts) + ([prev] if prev is not None else [])
    shape = (parts[0].shape[1], parts[0].shape[2] * len(parts), parts[0].shape[3])
    return pl.pallas_call(
        functools.partial(term_kernel, len(parts), 1.0 if prev is None else 2.0),
        out_shape=jax.ShapeDtypeStruct(shape, parts[0].dtype),
        in_specs=[VM] * len(operands),
        out_specs=VM,
    )(*operands)


def spread_out(piece, axes):
    size = lax.axis_size(axes)
    return lax.all_to_all(jnp.broadcast_to(piece, (size,) + piece.shape), axes, 0, 0, tiled=True)


def merge(stats, axes, nodes):
    gathered = spread_out(stats, axes)
    means, squares = gathered[:, :2], gathered[:, 2:]
    mean = jnp.mean(means, axis=0)
    off = means - mean[None]
    return jnp.concatenate([mean, jnp.sum(squares + nodes * (off * off), axis=0)], axis=0)


def local(features, tiles, tile_rows, tile_count, filters):
    piece, width = features.shape
    hid_width = filters.shape[2]
    z_size, y_size, x_size = lax.axis_size("z"), lax.axis_size("y"), lax.axis_size("x")
    x_index = lax.axis_index("x")

    y_first = {"yz": (True,), "zy": (False,), "split": (True, False)}[MODE]
    rows = piece // len(y_first)
    matrices = []
    for dense in place(tiles, tile_rows, tile_count, z_size, y_size, piece, y_first):
        swapped = lax.all_to_all(dense, "core", 0, 0, tiled=True)
        matrices.append(jnp.concatenate([swapped[0], swapped[1]], axis=-1).reshape(-1, 2 * tiles.shape[2]))

    def propagate(vector, copies):
        parts = []
        for y, matrix in zip(y_first, matrices):
            one, two = ("y", "z") if y else ("z", "y")
            products = jnp.dot(matrix, vector, preferred_element_type=jnp.float32).astype(jnp.bfloat16)
            products = products.reshape(lax.axis_size(one), lax.axis_size(two), rows, width)
            received = lax.all_to_all(products, one, 0, 0, tiled=True)
            summed = sum_sources(received, copies)
            summed = summed.reshape(-1, rows, width)
            received = lax.all_to_all(summed, (two, "x") if copies > 1 else two, 0, 0, tiled=True)
            parts.append(received.reshape(lax.axis_size(two), copies, rows, width))
        return parts

    def both_cores(half):
        return lax.all_gather(half.reshape(-1, width), "core", axis=0, tiled=True)

    def own(array):
        return lax.dynamic_index_in_dim(array, x_index, 0, keepdims=False)

    gathered = spread_out(features, ("core", "x"))
    half0 = lax.dynamic_slice_in_dim(gathered, lax.axis_index("core") * x_size, x_size, 0)
    half1 = next_term(propagate(gathered.reshape(-1, width), x_size), None)
    half2 = next_term(propagate(both_cores(half1), x_size), half0)
    own1 = own(half1)
    term3 = next_term(propagate(both_cores(half2), 1), own1[None])[0]
    stacked = jnp.concatenate([features, own1, own(half2), term3], axis=1)
    hidden = jnp.dot(stacked, filters.reshape(-1, hid_width), preferred_element_type=jnp.float32)

    mean = jnp.mean(hidden, axis=0)
    off = hidden - mean[None, :]
    stats = jnp.stack([mean, jnp.sum(off * off, axis=0)]).reshape(4, hid_width // 2)
    nodes = piece
    for axes in ("y", "z", ("core", "x")):
        stats = merge(stats, axes, float(nodes))
        nodes = nodes * lax.axis_size(axes)
    spread = jnp.sum(stats[2:]) / nodes
    centered = hidden - stats[:2].reshape(1, hid_width)
    return (centered * lax.rsqrt(spread + epsilon)).astype(jnp.bfloat16)


def split_of(row_devices):
    y_size = 8
    return row_devices // (2 * y_size), y_size


def solution(mesh):
    cols = mesh.shape["col"]
    z_size, y_size = split_of(mesh.shape["row"])
    fine = Mesh(mesh.devices.reshape(z_size, y_size, 2, cols), ("z", "y", "core", "x"))
    rows = ("z", "y", "core", "x")
    return jax.shard_map(
        local,
        mesh=fine,
        in_specs=(P(rows, None), P(rows, None, None), P(rows), P(rows), P()),
        out_specs=P(rows, None),
        check_vma=False,
    )
```

```python
import jax
import jax.numpy as jnp
from jax import lax
from jax.experimental import pallas as pl
from jax.experimental.pallas import tpu as pltpu
from jax.sharding import Mesh
from jax.sharding import PartitionSpec as P

VM = pl.BlockSpec(memory_space=pltpu.VMEM)
SM = pl.BlockSpec(memory_space=pltpu.SMEM)
CORES = 2
ALL = "device"
epsilon = 1e-05


class Layout:
    def __init__(self, zs, ys, xs):
        self.zs, self.ys, self.xs = zs, ys, xs
        self.members = 2 * 2 * CORES
        self.squares = zs * ys // 4
        at = lambda z, y, core, x: ((z * ys + y) * CORES + core) * xs + x
        Z, Y, C, X, B = range(zs), range(ys), range(CORES), range(xs), range(2)
        corners = [(z, y) for z in range(0, zs, 2) for y in range(0, ys, 2)]
        member = [(core, y, z) for core in C for y in B for z in B]
        self.square = [[at(z + j, y + i, core, x) for core, i, j in member] for z, y in corners for x in X]
        self.square_line = [[at(z + j, y + i, core, x) for core, i, j in member for x in X] for z, y in corners]
        self.across = [[at(z + j, y + i, core, x) for z, y in corners] for core, i, j in member for x in X]
        self.y_x = [[at(z, y, core, x) for y in Y for x in X] for z in Z for core in C]
        self.z_core = [[at(z, y, core, x) for z in Z for core in C] for y in Y for x in X]

    def place_of(self, core, chip):
        z, y = chip // self.ys, chip % self.ys
        return (core * 2 + y % 2) * 2 + z % 2, (z // 2) * (self.ys // 2) + y // 2


def exchange(array, groups):
    return lax.all_to_all(array, ALL, 0, 0, axis_index_groups=groups, tiled=True)


def place(layout, tiles, tile_rows, tile_count, piece):
    def kernel(rows_ref, count_ref, tiles_ref, out_ref):
        pieces = tiles_ref.shape[1] // piece
        out_ref[...] = jnp.zeros_like(out_ref)

        def put(slot, carry):
            first = rows_ref[slot] * pieces
            for q in range(pieces):
                member, square = layout.place_of(q % CORES, (first + q) // CORES)
                out_ref[member, square] = tiles_ref[slot, q * piece : (q + 1) * piece, :]
            return carry

        lax.fori_loop(0, count_ref[0], put, 0)

    return pl.pallas_call(
        kernel,
        out_shape=jax.ShapeDtypeStruct((layout.members, layout.squares, piece, tiles.shape[2]), tiles.dtype),
        in_specs=[SM, SM, VM],
        out_specs=VM,
        compiler_params=pltpu.CompilerParams(vmem_limit_bytes=16 * 1024 * 1024),
    )(tile_rows, tile_count, tiles)


def total_of(ref, *at):
    total = ref[(0, *at)].astype(jnp.float32)
    for source in range(1, ref.shape[0]):
        total = total + ref[(source, *at)].astype(jnp.float32)
    return total


def next_term(partial, prev, copies):
    def kernel(in_ref, *refs):
        out_ref = refs[-1]
        term = total_of(in_ref)
        if prev is not None:
            term = 2.0 * term - refs[0][...].astype(jnp.float32)
        for copy in range(copies):
            out_ref[copy] = term.astype(out_ref.dtype)

    operands = [partial] if prev is None else [partial, prev]
    return pl.pallas_call(
        kernel,
        out_shape=jax.ShapeDtypeStruct((copies,) + partial.shape[1:], partial.dtype),
        in_specs=[VM] * len(operands),
        out_specs=VM,
    )(*operands)


def merge(stats, groups, nodes):
    gathered = exchange(jnp.broadcast_to(stats, (len(groups[0]),) + stats.shape), groups)
    means, squares = gathered[:, :2], gathered[:, 2:]
    mean = jnp.mean(means, axis=0)
    off = means - mean[None]
    return jnp.concatenate([mean, jnp.sum(squares + nodes * (off * off), axis=0)], axis=0)


def local_of(layout):
    def local(features, tiles, tile_rows, tile_count, filters):
        piece, width = features.shape
        hid_width = filters.shape[2]
        copies = layout.members * layout.xs

        def gather(pieces):
            return exchange(pieces, layout.square_line).reshape(-1, width)

        vector = gather(jnp.broadcast_to(features, (copies,) + features.shape))
        dense = place(layout, tiles, tile_rows, tile_count, piece)
        dense, vector = lax.optimization_barrier((dense, vector))
        swapped = exchange(dense, layout.square).reshape(layout.members, -1, tiles.shape[2])
        matrix = jnp.concatenate([swapped[i] for i in range(layout.members)], axis=-1)

        def propagate(vector):
            products = jnp.dot(matrix, vector, preferred_element_type=jnp.float32).astype(jnp.bfloat16)
            return exchange(products.reshape(layout.squares, piece, width), layout.across)

        pieces1 = next_term(propagate(vector), None, copies)
        pieces2 = next_term(propagate(gather(pieces1)), features, copies)
        term3 = next_term(propagate(gather(pieces2)), pieces1[0], 1)[0]
        stacked = jnp.concatenate([features, pieces1[0], pieces2[0], term3], axis=1)
        hidden = jnp.dot(stacked, filters.reshape(-1, hid_width), preferred_element_type=jnp.float32)

        mean = jnp.mean(hidden, axis=0)
        off = hidden - mean[None, :]
        stats = jnp.stack([mean, jnp.sum(off * off, axis=0)]).reshape(4, hid_width // 2)
        nodes = piece
        for groups in (layout.y_x, layout.z_core):
            stats = merge(stats, groups, float(nodes))
            nodes = nodes * len(groups[0])
        spread = jnp.sum(stats[2:]) / nodes
        centered = hidden - stats[:2].reshape(1, hid_width)
        return (centered * lax.rsqrt(spread + epsilon)).astype(jnp.bfloat16)

    return local


def split_of(row_devices):
    return row_devices // (8 * CORES), 8


def solution(mesh):
    zs, ys = split_of(mesh.shape["row"])
    line = Mesh(mesh.devices.reshape(-1), (ALL,))
    return jax.shard_map(
        local_of(Layout(zs, ys, mesh.shape["col"])),
        mesh=line,
        in_specs=(P(ALL, None), P(ALL, None, None), P(ALL), P(ALL), P()),
        out_specs=P(ALL, None),
        check_vma=False,
    )
```

```python
import jax
import jax.numpy as jnp
from jax import lax
from jax.experimental import pallas as pl
from jax.experimental.pallas import tpu as pltpu
from jax.sharding import Mesh
from jax.sharding import PartitionSpec as P

VM = pl.BlockSpec(memory_space=pltpu.VMEM)
SM = pl.BlockSpec(memory_space=pltpu.SMEM)
CORES = 2
ALL = "device"
epsilon = 1e-05


class Layout:
    def __init__(self, zs, ys, xs):
        self.zs, self.ys, self.xs = zs, ys, xs
        self.members = 2 * 2 * CORES
        self.squares = zs * ys // 4
        at = lambda z, y, core, x: ((z * ys + y) * CORES + core) * xs + x
        Z, Y, C, X, B = range(zs), range(ys), range(CORES), range(xs), range(2)
        corners = [(z, y) for z in range(0, zs, 2) for y in range(0, ys, 2)]
        member = [(core, y, z) for core in C for y in B for z in B]
        self.square = [[at(z + j, y + i, core, x) for core, i, j in member] for z, y in corners for x in X]
        self.square_line = [[at(z + j, y + i, core, x) for core, i, j in member for x in X] for z, y in corners]
        self.across = [[at(z + j, y + i, core, x) for z, y in corners] for core, i, j in member for x in X]
        self.y_x = [[at(z, y, core, x) for y in Y for x in X] for z in Z for core in C]
        self.z_core = [[at(z, y, core, x) for z in Z for core in C] for y in Y for x in X]

    def place_of(self, core, chip):
        z, y = chip // self.ys, chip % self.ys
        return (core * 2 + y % 2) * 2 + z % 2, (z // 2) * (self.ys // 2) + y // 2


def exchange(array, groups):
    return lax.all_to_all(array, ALL, 0, 0, axis_index_groups=groups, tiled=True)


def place(layout, tiles, tile_rows, tile_count, piece):
    def kernel(rows_ref, count_ref, tiles_ref, out_ref):
        pieces = tiles_ref.shape[1] // piece
        out_ref[...] = jnp.zeros_like(out_ref)

        def put(slot, carry):
            first = rows_ref[slot] * pieces
            for q in range(pieces):
                member, square = layout.place_of(q % CORES, (first + q) // CORES)
                out_ref[member, square] = tiles_ref[slot, q * piece : (q + 1) * piece, :]
            return carry

        lax.fori_loop(0, count_ref[0], put, 0)

    return pl.pallas_call(
        kernel,
        out_shape=jax.ShapeDtypeStruct((layout.members, layout.squares, piece, tiles.shape[2]), tiles.dtype),
        in_specs=[SM, SM, VM],
        out_specs=VM,
        compiler_params=pltpu.CompilerParams(vmem_limit_bytes=16 * 1024 * 1024),
    )(tile_rows, tile_count, tiles)


def next_term(partial, prev):
    term = partial[0].astype(jnp.float32)
    for source in range(1, partial.shape[0]):
        term = term + partial[source].astype(jnp.float32)
    if prev is not None:
        term = 2.0 * term - prev.astype(jnp.float32)
    return term.astype(partial.dtype)


def merge(stats, groups, nodes):
    gathered = exchange(jnp.broadcast_to(stats, (len(groups[0]),) + stats.shape), groups)
    means, squares = gathered[:, :2], gathered[:, 2:]
    mean = jnp.mean(means, axis=0)
    off = means - mean[None]
    return jnp.concatenate([mean, jnp.sum(squares + nodes * (off * off), axis=0)], axis=0)


def local_of(layout):
    def local(features, tiles, tile_rows, tile_count, filters):
        piece, width = features.shape
        hid_width = filters.shape[2]
        copies = layout.members * layout.xs

        def gather(piece_rows):
            pieces = jnp.broadcast_to(piece_rows, (copies,) + piece_rows.shape)
            return exchange(pieces, layout.square_line).reshape(-1, width)

        vector = gather(features)
        dense = place(layout, tiles, tile_rows, tile_count, piece)
        dense, vector = lax.optimization_barrier((dense, vector))
        swapped = exchange(dense, layout.square).reshape(layout.members, -1, tiles.shape[2])
        matrix = jnp.concatenate([swapped[i] for i in range(layout.members)], axis=-1)

        def propagate(vector):
            products = jnp.dot(matrix, vector, preferred_element_type=jnp.float32).astype(jnp.bfloat16)
            return exchange(products.reshape(layout.squares, piece, width), layout.across)

        term1 = next_term(propagate(vector), None)
        term2 = next_term(propagate(gather(term1)), features)
        term3 = next_term(propagate(gather(term2)), term1)
        stacked = jnp.concatenate([features, term1, term2, term3], axis=1)
        hidden = jnp.dot(stacked, filters.reshape(-1, hid_width), preferred_element_type=jnp.float32)

        mean = jnp.mean(hidden, axis=0)
        off = hidden - mean[None, :]
        stats = jnp.stack([mean, jnp.sum(off * off, axis=0)]).reshape(4, hid_width // 2)
        nodes = piece
        for groups in (layout.y_x, layout.z_core):
            stats = merge(stats, groups, float(nodes))
            nodes = nodes * len(groups[0])
        spread = jnp.sum(stats[2:]) / nodes
        centered = hidden - stats[:2].reshape(1, hid_width)
        return (centered * lax.rsqrt(spread + epsilon)).astype(jnp.bfloat16)

    return local


def split_of(row_devices):
    return row_devices // (8 * CORES), 8


def solution(mesh):
    zs, ys = split_of(mesh.shape["row"])
    line = Mesh(mesh.devices.reshape(-1), (ALL,))
    return jax.shard_map(
        local_of(Layout(zs, ys, mesh.shape["col"])),
        mesh=line,
        in_specs=(P(ALL, None), P(ALL, None, None), P(ALL), P(ALL), P()),
        out_specs=P(ALL, None),
        check_vma=False,
    )
```

```python
import jax
import jax.numpy as jnp
from jax import lax
from jax.experimental import pallas as pl
from jax.experimental.pallas import tpu as pltpu
from jax.sharding import Mesh
from jax.sharding import PartitionSpec as P

VM = pl.BlockSpec(memory_space=pltpu.VMEM)
SM = pl.BlockSpec(memory_space=pltpu.SMEM)
CORES = 2
ALL = "device"
epsilon = 1e-05


class Layout:
    def __init__(self, zs, ys, xs):
        self.zs, self.ys, self.xs = zs, ys, xs
        self.members = 2 * 2 * CORES
        self.squares = zs * ys // 4
        at = lambda z, y, core, x: ((z * ys + y) * CORES + core) * xs + x
        Z, Y, C, X, B = range(zs), range(ys), range(CORES), range(xs), range(2)
        corners = [(z, y) for y in range(0, ys, 2) for z in range(0, zs, 2)]
        member = [(core, y, z) for core in C for y in B for z in B]
        self.square = [[at(z + j, y + i, core, x) for core, i, j in member] for z, y in corners for x in X]
        self.x_line = [[at(z, y, core, x) for x in X] for z in Z for y in Y for core in C]
        self.square_line = [[at(z + j, y + i, core, x) for core, i, j in member for x in X] for z, y in corners]
        self.across = [[at(z + j, y + i, core, x) for z, y in corners] for core, i, j in member for x in X]
        self.y_x = [[at(z, y, core, x) for y in Y for x in X] for z in Z for core in C]
        self.z_core = [[at(z, y, core, x) for z in Z for core in C] for y in Y for x in X]

    def place_of(self, core, chip):
        z, y = chip // self.ys, chip % self.ys
        return (core * 2 + y % 2) * 2 + z % 2, (y // 2) * (self.zs // 2) + z // 2


def exchange(array, groups):
    return lax.all_to_all(array, ALL, 0, 0, axis_index_groups=groups, tiled=True)


def place(layout, tiles, tile_rows, tile_count, piece):
    def kernel(rows_ref, count_ref, tiles_ref, out_ref):
        pieces = tiles_ref.shape[1] // piece
        out_ref[...] = jnp.zeros_like(out_ref)

        def put(slot, carry):
            first = rows_ref[slot] * pieces
            for q in range(pieces):
                member, square = layout.place_of(q % CORES, (first + q) // CORES)
                out_ref[member, square] = tiles_ref[slot, q * piece : (q + 1) * piece, :]
            return carry

        lax.fori_loop(0, count_ref[0], put, 0)

    return pl.pallas_call(
        kernel,
        out_shape=jax.ShapeDtypeStruct((layout.members, layout.squares, piece, tiles.shape[2]), tiles.dtype),
        in_specs=[SM, SM, VM],
        out_specs=VM,
        compiler_params=pltpu.CompilerParams(vmem_limit_bytes=16 * 1024 * 1024),
    )(tile_rows, tile_count, tiles)


def next_term(partial, prev):
    term = partial[0].astype(jnp.float32)
    for source in range(1, partial.shape[0]):
        term = term + partial[source].astype(jnp.float32)
    if prev is not None:
        term = 2.0 * term - prev.astype(jnp.float32)
    return term.astype(partial.dtype)


def merge(stats, groups, nodes):
    gathered = exchange(jnp.broadcast_to(stats, (len(groups[0]),) + stats.shape), groups)
    means, squares = gathered[:, :2], gathered[:, 2:]
    mean = jnp.mean(means, axis=0)
    off = means - mean[None]
    return jnp.concatenate([mean, jnp.sum(squares + nodes * (off * off), axis=0)], axis=0)


def local_of(layout):
    def local(features, tiles, tile_rows, tile_count, filters):
        piece, width = features.shape
        hid_width = filters.shape[2]
        copies = layout.members * layout.xs

        def gather(piece_rows):
            pieces = jnp.broadcast_to(piece_rows, (copies,) + piece_rows.shape)
            return exchange(pieces, layout.square_line).reshape(-1, width)

        in_square = jnp.broadcast_to(features, (layout.members,) + features.shape)
        in_square = exchange(in_square, layout.square)
        dense = place(layout, tiles, tile_rows, tile_count, piece)
        dense, in_square = lax.optimization_barrier((dense, in_square))
        vector = lax.all_gather(in_square, ALL, axis=0, axis_index_groups=layout.x_line)
        vector = jnp.swapaxes(vector, 0, 1).reshape(-1, width)
        swapped = exchange(dense, layout.square).reshape(layout.members, -1, tiles.shape[2])
        matrix = jnp.concatenate([swapped[i] for i in range(layout.members)], axis=-1)

        def propagate(vector):
            products = jnp.dot(matrix, vector, preferred_element_type=jnp.float32).astype(jnp.bfloat16)
            return exchange(products.reshape(layout.squares, piece, width), layout.across)

        term1 = next_term(propagate(vector), None)
        term2 = next_term(propagate(gather(term1)), features)
        term3 = next_term(propagate(gather(term2)), term1)
        stacked = jnp.concatenate([features, term1, term2, term3], axis=1)
        hidden = jnp.dot(stacked, filters.reshape(-1, hid_width), preferred_element_type=jnp.float32)

        mean = jnp.mean(hidden, axis=0)
        off = hidden - mean[None, :]
        stats = jnp.stack([mean, jnp.sum(off * off, axis=0)]).reshape(4, hid_width // 2)
        nodes = piece
        for groups in (layout.y_x, layout.z_core):
            stats = merge(stats, groups, float(nodes))
            nodes = nodes * len(groups[0])
        spread = jnp.sum(stats[2:]) / nodes
        centered = hidden - stats[:2].reshape(1, hid_width)
        return (centered * lax.rsqrt(spread + epsilon)).astype(jnp.bfloat16)

    return local


def split_of(row_devices):
    return row_devices // (8 * CORES), 8


def solution(mesh):
    zs, ys = split_of(mesh.shape["row"])
    line = Mesh(mesh.devices.reshape(-1), (ALL,))
    return jax.shard_map(
        local_of(Layout(zs, ys, mesh.shape["col"])),
        mesh=line,
        in_specs=(P(ALL, None), P(ALL, None, None), P(ALL), P(ALL), P()),
        out_specs=P(ALL, None),
        check_vma=False,
    )
```

```python
import jax
import jax.numpy as jnp
from jax import lax
from jax.experimental import pallas as pl
from jax.experimental.pallas import tpu as pltpu
from jax.sharding import Mesh
from jax.sharding import PartitionSpec as P

ANY = pl.BlockSpec(memory_space=pl.ANY)
VM = pl.BlockSpec(memory_space=pltpu.VMEM)
SM = pl.BlockSpec(memory_space=pltpu.SMEM)
CORES = 2
ALL = "device"
epsilon = 1e-05


class Layout:
    def __init__(self, zs, ys, xs):
        self.zs, self.ys, self.xs = zs, ys, xs
        self.members = 2 * 2 * CORES
        self.squares = zs * ys // 4
        at = lambda z, y, core, x: ((z * ys + y) * CORES + core) * xs + x
        Z, Y, C, X, B = range(zs), range(ys), range(CORES), range(xs), range(2)
        corners = [(z, y) for y in range(0, ys, 2) for z in range(0, zs, 2)]
        member = [(core, y, z) for core in C for y in B for z in B]
        self.square = [[at(z + j, y + i, core, x) for core, i, j in member] for z, y in corners for x in X]
        self.x_line = [[at(z, y, core, x) for x in X] for z in Z for y in Y for core in C]
        self.square_line = [[at(z + j, y + i, core, x) for core, i, j in member for x in X] for z, y in corners]
        self.across = [[at(z + j, y + i, core, x) for z, y in corners] for core, i, j in member for x in X]
        self.y_x = [[at(z, y, core, x) for y in Y for x in X] for z in Z for core in C]
        self.z_core = [[at(z, y, core, x) for z in Z for core in C] for y in Y for x in X]

    def place_of(self, core, chip):
        z, y = chip // self.ys, chip % self.ys
        return (core * 2 + y % 2) * 2 + z % 2, (y // 2) * (self.zs // 2) + z // 2


def exchange(array, groups):
    return lax.all_to_all(array, ALL, 0, 0, axis_index_groups=groups, tiled=True)


def place(layout, tiles, tile_rows, tile_count, piece):
    def kernel(rows_ref, count_ref, from_ref, out_ref, tiles_ref, sem):
        pieces = tiles_ref.shape[1] // piece
        fetch = pltpu.make_async_copy(from_ref, tiles_ref, sem)
        fetch.start()
        out_ref[...] = jnp.zeros_like(out_ref)
        fetch.wait()

        def put(slot, carry):
            first = rows_ref[slot] * pieces
            for q in range(pieces):
                member, square = layout.place_of(q % CORES, (first + q) // CORES)
                out_ref[member, square] = tiles_ref[slot, q * piece : (q + 1) * piece, :]
            return carry

        lax.fori_loop(0, count_ref[0], put, 0)

    return pl.pallas_call(
        kernel,
        out_shape=jax.ShapeDtypeStruct((layout.members, layout.squares, piece, tiles.shape[2]), tiles.dtype),
        in_specs=[SM, SM, ANY],
        out_specs=VM,
        scratch_shapes=[pltpu.VMEM(tiles.shape, tiles.dtype), pltpu.SemaphoreType.DMA],
        compiler_params=pltpu.CompilerParams(vmem_limit_bytes=60 * 1024 * 1024),
    )(tile_rows, tile_count, tiles)


def next_term(partial, prev):
    term = partial[0].astype(jnp.float32)
    for source in range(1, partial.shape[0]):
        term = term + partial[source].astype(jnp.float32)
    if prev is not None:
        term = 2.0 * term - prev.astype(jnp.float32)
    return term.astype(partial.dtype)


def merge(stats, groups, nodes):
    gathered = exchange(jnp.broadcast_to(stats, (len(groups[0]),) + stats.shape), groups)
    means, squares = gathered[:, :2], gathered[:, 2:]
    mean = jnp.mean(means, axis=0)
    off = means - mean[None]
    return jnp.concatenate([mean, jnp.sum(squares + nodes * (off * off), axis=0)], axis=0)


def local_of(layout):
    def local(features, tiles, tile_rows, tile_count, filters):
        piece, width = features.shape
        hid_width = filters.shape[2]
        copies = layout.members * layout.xs

        def gather(piece_rows):
            pieces = jnp.broadcast_to(piece_rows, (copies,) + piece_rows.shape)
            return exchange(pieces, layout.square_line).reshape(-1, width)

        in_square = jnp.broadcast_to(features, (layout.members,) + features.shape)
        in_square = exchange(in_square, layout.square)
        dense = place(layout, tiles, tile_rows, tile_count, piece)
        dense, in_square = lax.optimization_barrier((dense, in_square))
        vector = lax.all_gather(in_square, ALL, axis=0, axis_index_groups=layout.x_line)
        vector = jnp.swapaxes(vector, 0, 1).reshape(-1, width)
        swapped = exchange(dense, layout.square).reshape(layout.members, -1, tiles.shape[2])
        matrix = jnp.concatenate([swapped[i] for i in range(layout.members)], axis=-1)

        def propagate(vector):
            products = jnp.dot(matrix, vector, preferred_element_type=jnp.float32).astype(jnp.bfloat16)
            return exchange(products.reshape(layout.squares, piece, width), layout.across)

        term1 = next_term(propagate(vector), None)
        term2 = next_term(propagate(gather(term1)), features)
        term3 = next_term(propagate(gather(term2)), term1)
        stacked = jnp.concatenate([features, term1, term2, term3], axis=1)
        hidden = jnp.dot(stacked, filters.reshape(-1, hid_width), preferred_element_type=jnp.float32)

        mean = jnp.mean(hidden, axis=0)
        off = hidden - mean[None, :]
        stats = jnp.stack([mean, jnp.sum(off * off, axis=0)]).reshape(4, hid_width // 2)
        nodes = piece
        for groups in (layout.y_x, layout.z_core):
            stats = merge(stats, groups, float(nodes))
            nodes = nodes * len(groups[0])
        spread = jnp.sum(stats[2:]) / nodes
        centered = hidden - stats[:2].reshape(1, hid_width)
        return (centered * lax.rsqrt(spread + epsilon)).astype(jnp.bfloat16)

    return local


def split_of(row_devices):
    return row_devices // (8 * CORES), 8


def solution(mesh):
    zs, ys = split_of(mesh.shape["row"])
    line = Mesh(mesh.devices.reshape(-1), (ALL,))
    return jax.shard_map(
        local_of(Layout(zs, ys, mesh.shape["col"])),
        mesh=line,
        in_specs=(P(ALL, None), P(ALL, None, None), P(ALL), P(ALL), P()),
        out_specs=P(ALL, None),
        check_vma=False,
    )
```
